32 devices in a mesh: row: 8 (over z, core), col: 4 (over y, x).
Axes of the slice: x: 2, y: 2, z: 4, core: 2. Of those that a mesh axis runs over, the one named last changes fastest.
Arguments:
- gradient: bfloat16 [8192, 26624], P('row', 'col'), may hold values from -128 to 128
- momentum: bfloat16 [8192, 26624], P('row', 'col'), may hold values from -6 to 6
- weight: bfloat16 [8192, 26624], P('row', 'col'), may hold values from -6 to 6
- right_factor: float32 [26624, 256], P('col'), may hold values from -6 to 6
Outputs:
- new_weight: bfloat16 [8192, 26624], P('row', 'col')
- new_momentum: bfloat16 [8192, 26624], P('row', 'col')
- new_factor: float32 [26624, 256], P('col')
The draws below stay inside these ranges and needn't reach their ends.
All inputs are finite; a program needn't handle non-finite values.
Results may differ from the reference program's by a relative error of at most 0.0015.
Values sent between devices are 32-bit elements; how exact they have to be, the bound alone decides.
A program may use at most 128 MiB of HBM per device.

```python
import math
import jax
import jax.numpy as jnp
from jax import lax

ROWS = 8192
COLS = 26624
RANK = 256


def draw_gradient(key, part):
    key = jax.random.fold_in(key, 11)
    keys = jax.random.split(key, 7)
    row_scale = jnp.exp(jax.random.uniform(keys[0], (ROWS, 1), jnp.float32, math.log(0.3), math.log(3.0)))
    col_index = jnp.arange(COLS, dtype=jnp.float32)[None, :]
    col_scale = jnp.exp(jax.random.uniform(keys[1], (1, COLS), jnp.float32, math.log(0.5), math.log(2.0)) + math.log(3.0) * col_index / COLS)
    factors = max(RANK // 4, 1)
    base = jax.random.truncated_normal(keys[2], -4.0, 4.0, (ROWS, COLS), jnp.float32)
    row_vectors = jax.random.truncated_normal(keys[5], -4.0, 4.0, (ROWS, factors), jnp.float32)
    col_vectors = jax.random.truncated_normal(keys[6], -4.0, 4.0, (factors, COLS), jnp.float32)
    strength = 3.0
    lowrank = jnp.dot(row_vectors, col_vectors, precision=lax.Precision.HIGHEST) * (strength / math.sqrt(factors))
    return jnp.clip((base + lowrank) * row_scale * col_scale, -128.0, 128.0).astype(jnp.bfloat16)


def levels(rng, dims, pieces, low, top_value):
    def one(axis_at, parts):
        steps = jax.random.uniform(jax.random.fold_in(jax.random.fold_in(rng, 6), axis_at), (parts,), jnp.float32, low / len(pieces), top_value / len(pieces))
        return jnp.repeat(jnp.exp(steps), dims[axis_at] // parts).reshape((-1,) + (1,) * (len(dims) - axis_at - 1))

    level = one(*pieces[0])
    for cut in pieces[1:]:
        level = level * one(*cut)
    return level


def centred(rng, extent, scale, most, pieces=(), kind=jnp.bfloat16):
    gain = levels(rng, extent, pieces, -0.22, 0.18) if pieces else 1.0
    drawn = jax.random.normal(rng, extent, jnp.float32) * scale * gain
    return jnp.minimum(jnp.maximum(drawn, -most), most).astype(kind)


def setup_inputs(seed: int = 0) -> dict:
    key_list = jax.random.split(jax.random.key(seed), 5)
    gradient = draw_gradient(jax.random.fold_in(key_list[4], 71), 0)
    momentum = centred(key_list[1], (ROWS, COLS), 1.0, 6.0, ((0, 8), (1, 4)))
    weight = centred(key_list[2], (ROWS, COLS), 1.0, 6.0, ((0, 8), (1, 4)))
    right_factor = centred(key_list[3], (COLS, RANK), 1.0, 6.0, ((0, 4),), jnp.float32)
    return dict(gradient=gradient, momentum=momentum, weight=weight, right_factor=right_factor)


decay = 0.95
step_size = 0.3

def factor_gram(gram):
    jitter = 1e-06 * jnp.trace(gram) / RANK
    return jnp.linalg.cholesky(gram + jitter * jnp.eye(RANK, dtype=jnp.float32))

def solve_right(block, chol):
    return lax.linalg.triangular_solve(chol, block, left_side=False, lower=True, transpose_a=True)

def reference(gradient, momentum, weight, right_factor):
    high = lax.Precision.HIGHEST
    buffer = momentum.astype(jnp.float32) + gradient.astype(jnp.float32)
    left = jnp.dot(buffer, right_factor, precision=high)
    gram = jnp.dot(left.T, left, precision=high)
    chol = factor_gram(gram)
    ortho = solve_right(left, chol)
    right = lax.dot_general(buffer, ortho, (((0,), (0,)), ((), ())), precision=high)
    new_momentum = (buffer - (1.0 - decay) * jnp.dot(ortho, right.T, precision=high)).astype(jnp.bfloat16)
    squares = lax.optimization_barrier(jnp.sum(right * right, axis=0))
    new_factor = right / jnp.sqrt(squares / COLS + 1e-06)
    update = jnp.dot(ortho, new_factor.T, precision=high)
    new_weight = (weight.astype(jnp.float32) - step_size * jnp.sqrt(ROWS / RANK) * update).astype(jnp.bfloat16)
    return (new_weight, new_momentum, new_factor)
```

```python
import functools

import jax
import jax.numpy as jnp
from jax import lax
from jax.experimental import pallas as pl
from jax.experimental.pallas import tpu as pltpu
from jax.sharding import PartitionSpec as P

ROWS = 8192
COLS = 26624
RANK = 256

decay = 0.95
step_size = 0.3

MESH = pl.DeviceIdType.MESH
HIGH = lax.Precision.HIGHEST
F32 = jnp.float32
BF16 = jnp.bfloat16
VMEM = pltpu.VMEM
DMA = pltpu.SemaphoreType.DMA
LIMIT = 56 * 1024 * 1024


def split(x):
    hi = x.astype(BF16)
    return hi, (x - hi.astype(F32)).astype(BF16)


def mm(a, b):
    return jnp.dot(a, b, preferred_element_type=F32)


def tile_of(cols):
    for tile in (512, 256, 128):
        if cols % tile == 0:
            return tile
    return cols


def whole(shape):
    return pl.BlockSpec(shape, lambda i: (0,) * len(shape))


def left_kernel(g_ref, m_ref, r_ref, out_ref):
    @pl.when(pl.program_id(0) == 0)
    def _():
        out_ref[...] = jnp.zeros_like(out_ref)

    b_hi, b_lo = split(g_ref[...].astype(F32) + m_ref[...].astype(F32))
    r_hi, r_lo = split(r_ref[...])
    out_ref[...] += mm(b_hi, r_hi) + mm(b_lo, r_hi) + mm(b_hi, r_lo)


def left_part(g, m, r):
    rows, cols = g.shape
    tile = tile_of(cols)
    return pl.pallas_call(
        left_kernel,
        grid=(cols // tile,),
        in_specs=[
            pl.BlockSpec((rows, tile), lambda i: (0, i)),
            pl.BlockSpec((rows, tile), lambda i: (0, i)),
            pl.BlockSpec((tile, RANK), lambda i: (i, 0)),
        ],
        out_specs=whole((rows, RANK)),
        out_shape=jax.ShapeDtypeStruct((rows, RANK), F32),
        compiler_params=pltpu.CompilerParams(vmem_limit_bytes=LIMIT),
    )(g, m, r)


def greet(peers):
    barrier = pltpu.get_barrier_semaphore()
    for peer in peers:
        pl.semaphore_signal(barrier, inc=1, device_id=peer, device_id_type=MESH)
    return barrier


def sums_kernel(nr, nc, part, left, gram, l_in, g_part, g_in, ls, lr, las, lar, gs, gr, gas, gar):
    ri, ci = lax.axis_index("row"), lax.axis_index("col")
    cols = [lax.rem(ci + d, nc) for d in range(nc)]
    rows = [lax.rem(ri + d, nr) for d in range(nr)]
    barrier = greet([{"col": p} for p in cols[1:]] + [{"row": p} for p in rows[1:]])
    pl.semaphore_wait(barrier, nc + nr - 2)

    def copy(src, dst, send, recv, peer):
        return pltpu.make_async_remote_copy(
            src_ref=src, dst_ref=dst, send_sem=send, recv_sem=recv, device_id=peer, device_id_type=MESH
        )

    def reduce_gather(axis, n, me, others, src, slots, total, s1, r1, s2, r2):
        first = [
            copy(src.at[others[d]], slots.at[d - 1], s1.at[d - 1], r1.at[d - 1], {axis: others[d]})
            for d in range(1, n)
        ]
        for c in first:
            c.start()
        acc = src[me]
        for d in range(1, n):
            first[d - 1].wait_recv()
            acc = acc + slots[d - 1]
        total[me] = acc
        second = [
            copy(total.at[me], total.at[me], s2.at[d - 1], r2.at[d - 1], {axis: others[d]})
            for d in range(1, n)
        ]
        for c in second:
            c.start()
        for d in range(1, n):
            owner = lax.rem(me + n - d, n)
            copy(total.at[owner], total.at[owner], s2.at[d - 1], r2.at[d - 1], {axis: others[d]}).wait_recv()
        for c in first + second:
            c.wait_send()

    reduce_gather("col", nc, ci, cols, part, l_in, left, ls, lr, las, lar)
    total = jnp.zeros((RANK, RANK), F32)
    for k in range(nc):
        block = left[k]
        total += jnp.dot(block.T, block, precision=HIGH, preferred_element_type=F32)
    g_part[...] = total.reshape(g_part.shape)
    reduce_gather("row", nr, ri, rows, g_part, g_in, gram, gs, gr, gas, gar)


def sums(part, nr, nc):
    rows = part.shape[0]
    piece, gpiece = rows // nc, RANK // nr
    vm = pl.BlockSpec(memory_space=VMEM)
    left, gram = pl.pallas_call(
        functools.partial(sums_kernel, nr, nc),
        in_specs=[vm],
        out_specs=[vm, vm],
        out_shape=[
            jax.ShapeDtypeStruct((nc, piece, RANK), F32),
            jax.ShapeDtypeStruct((nr, gpiece, RANK), F32),
        ],
        scratch_shapes=[
            VMEM((nc - 1, piece, RANK), F32),
            VMEM((nr, gpiece, RANK), F32),
            VMEM((nr - 1, gpiece, RANK), F32),
        ]
        + [DMA((nc - 1,))] * 4
        + [DMA((nr - 1,))] * 4,
        compiler_params=pltpu.CompilerParams(
            collective_id=0, has_side_effects=True, vmem_limit_bytes=LIMIT
        ),
    )(part.reshape(nc, piece, RANK))
    return left.reshape(rows, RANK), gram.reshape(RANK, RANK)


def ortho_kernel(gram_ref, left_ref, hi_ref, lo_ref, t_ref, work, inv):
    nb = 32
    gram = gram_ref[...]
    eye = lax.broadcasted_iota(jnp.int32, (RANK, RANK), 0) == lax.broadcasted_iota(
        jnp.int32, (RANK, RANK), 1
    )
    trace = jnp.sum(jnp.sum(jnp.where(eye, gram, 0.0), axis=1, keepdims=True), axis=0, keepdims=True)
    work[:, :RANK] = gram + jnp.where(eye, 1e-06 * trace / RANK, 0.0)
    work[:, RANK:] = eye.astype(F32)
    inv[...] = jnp.zeros_like(inv)
    for r0 in range(0, RANK, nb):
        lo = 0 if r0 < 128 else 128
        width = 384
        panel = work[r0 : r0 + nb, lo : lo + width]
        row_id = lax.broadcasted_iota(jnp.int32, (nb, 1), 0)
        for j in range(nb):
            p = r0 + j - lo
            row = panel[j : j + 1, :]
            factor = panel[:, p : p + 1] / panel[j : j + 1, p : p + 1]
            panel = panel - jnp.where(row_id > j, factor, 0.0) * row
        lane = lax.broadcasted_iota(jnp.int32, (nb, width), 1)
        sub = lax.broadcasted_iota(jnp.int32, (nb, width), 0)
        pivots = jnp.sum(jnp.where(lane == sub + (r0 - lo), panel, 0.0), axis=1, keepdims=True)
        panel = panel / jnp.sqrt(pivots)
        inv[r0 : r0 + nb, 0 : lo + width - RANK] = panel[:, RANK - lo :]
        if r0 + nb < RANK:
            mult = panel[:, : RANK - lo].T
            mult = mult[r0 + nb - lo :, :]
            work[r0 + nb :, lo : lo + width] -= jnp.dot(
                mult, panel, precision=HIGH, preferred_element_type=F32
            )
    ortho = lax.dot_general(
        left_ref[...], inv[...], (((1,), (1,)), ((), ())), precision=HIGH, preferred_element_type=F32
    )
    hi, low = split(ortho)
    hi_ref[...] = hi
    lo_ref[...] = low
    hi, low = split(ortho.T)
    t_ref[:RANK, :] = hi
    t_ref[RANK:, :] = low


def ortho_of(gram, left):
    rows = left.shape[0]
    vm = pl.BlockSpec(memory_space=VMEM)
    return pl.pallas_call(
        ortho_kernel,
        in_specs=[vm, vm],
        out_specs=[vm, vm, vm],
        out_shape=[
            jax.ShapeDtypeStruct((rows, RANK), BF16),
            jax.ShapeDtypeStruct((rows, RANK), BF16),
            jax.ShapeDtypeStruct((2 * RANK, rows), BF16),
        ],
        scratch_shapes=[VMEM((RANK, 2 * RANK), F32), VMEM((RANK, RANK), F32)],
        compiler_params=pltpu.CompilerParams(vmem_limit_bytes=LIMIT),
    )(gram, left)


def right_kernel(g_ref, m_ref, t_ref, out_ref):
    b_hi, b_lo = split(g_ref[...].astype(F32) + m_ref[...].astype(F32))
    both = mm(t_ref[...], b_hi)
    out_ref[...] = both[:RANK] + both[RANK:] + mm(t_ref[:RANK, :], b_lo)


def right_part(g, m, t):
    rows, cols = g.shape
    tile = tile_of(cols)
    return pl.pallas_call(
        right_kernel,
        grid=(cols // tile,),
        in_specs=[
            pl.BlockSpec((rows, tile), lambda i: (0, i)),
            pl.BlockSpec((rows, tile), lambda i: (0, i)),
            whole((2 * RANK, rows)),
        ],
        out_specs=pl.BlockSpec((RANK, tile), lambda i: (0, i)),
        out_shape=jax.ShapeDtypeStruct((RANK, cols), F32),
        compiler_params=pltpu.CompilerParams(vmem_limit_bytes=LIMIT),
    )(g, m, t)


def total_kernel(nr, nc, x, out, sq, c_in, l_in, r_in, acc, sqs, cs, cr, rs, lr, rr, fl, fr, fz, ps, pr, ss, sr):
    nz = nr // 2
    half = x.shape[0] // 2
    ri, ci = lax.axis_index("row"), lax.axis_index("col")
    z, core = ri // 2, lax.rem(ri, 2)
    partner = ri + 1 - 2 * core
    mine, theirs = core * half, (1 - core) * half
    lower, upper = jnp.maximum(ri - 2, core), jnp.minimum(ri + 2, nr - 2 + core)
    cols = [lax.rem(ci + d, nc) for d in range(nc)]
    has_l, has_r = z > 0, z < nz - 1

    barrier = greet([{"row": partner}] + [{"col": p} for p in cols[1:]])

    @pl.when(has_l)
    def _():
        pl.semaphore_signal(barrier, inc=1, device_id={"row": lower}, device_id_type=MESH)

    @pl.when(has_r)
    def _():
        pl.semaphore_signal(barrier, inc=1, device_id={"row": upper}, device_id_type=MESH)

    pl.semaphore_wait(barrier, nc + jnp.minimum(z, 1) + jnp.minimum(nz - 1 - z, 1))

    def copy(src, dst, send, recv, peer, axis="row"):
        return pltpu.make_async_remote_copy(
            src_ref=src, dst_ref=dst, send_sem=send, recv_sem=recv, device_id={axis: peer}, device_id_type=MESH
        )

    def core_copy(s):
        return copy(x.at[theirs + s], c_in.at[s], cs.at[s], cr.at[s], partner)

    def up(s):
        return copy(acc.at[s], l_in.at[s], rs.at[s], lr.at[s], upper)

    def down(s):
        return copy(acc.at[s], r_in.at[s], rs.at[s], rr.at[s], lower)

    def final_down(s):
        return copy(out.at[mine + s], out.at[mine + s], fl.at[s], fz.at[s], lower)

    def final_up(s):
        return copy(out.at[mine + s], out.at[mine + s], fr.at[s], fz.at[s], upper)

    def share(s):
        return copy(out.at[mine + s], out.at[mine + s], ps.at[s], pr.at[s], partner)

    def share_in(s):
        return copy(out.at[theirs + s], out.at[theirs + s], ps.at[s], pr.at[s], partner)

    def centre(s):
        return nz // 2 - 1 + lax.rem(s, 2)

    def from_lower(s):
        @pl.when(has_l)
        def _():
            up(s).wait_recv()
            acc[s] += l_in[s]

    def from_upper(s):
        @pl.when(has_r)
        def _():
            down(s).wait_recv()
            acc[s] += r_in[s]

    def reduce(s):
        mid = centre(s)
        core_copy(s).wait_recv()
        acc[s] = x[mine + s] + c_in[s]

        @pl.when(z < mid)
        def _():
            from_lower(s)
            up(s).start()

        @pl.when(z > mid)
        def _():
            from_upper(s)
            down(s).start()

        @pl.when(z == mid)
        def _():
            from_lower(s)
            from_upper(s)
            out[mine + s] = acc[s]

            @pl.when(has_l)
            def _():
                final_down(s).start()

            @pl.when(has_r)
            def _():
                final_up(s).start()

            share(s).start()

    def spread(s):
        mid = centre(s)

        @pl.when(z < mid)
        def _():
            final_down(s).wait_recv()

            @pl.when(has_l)
            def _():
                final_down(s).start()

            share(s).start()

        @pl.when(z > mid)
        def _():
            final_up(s).wait_recv()

            @pl.when(has_r)
            def _():
                final_up(s).start()

            share(s).start()

    def loop(lo, hi, body):
        def step(s, carry):
            body(s)
            return carry

        lax.fori_loop(lo, hi, step, 0)

    loop(0, half, lambda s: core_copy(s).start())

    end = jnp.logical_or(z == 0, z == nz - 1)

    if nz > 2:

        @pl.when(end)
        def _():
            loop(0, half, reduce)
            loop(0, half, spread)

        @pl.when(jnp.logical_not(end))
        def _():
            loop(0, 2, reduce)

            def both(t):
                reduce(t)
                spread(t - 2)

            loop(2, half, both)
            loop(half - 2, half, spread)

    else:
        loop(0, half, reduce)
        loop(0, half, spread)

    lane = lax.broadcasted_iota(jnp.int32, (8, 128), 1)

    def square(i, carry):
        v = out[i]
        return carry + jnp.where(lane == i, jnp.sum(v * v, axis=1, keepdims=True), 0.0)

    def own(s, carry):
        return square(mine + s, carry)

    def other(s, carry):
        share_in(s).wait_recv()
        return square(theirs + s, carry)

    carry = lax.fori_loop(0, half, own, jnp.zeros((8, 128), F32))
    sqs[0] = lax.fori_loop(0, half, other, carry)
    sends = [copy(sqs.at[0], sqs.at[d], ss.at[d - 1], sr.at[d - 1], cols[d], "col") for d in range(1, nc)]
    for c in sends:
        c.start()

    def drain(s):
        mid = centre(s)
        core_copy(s).wait_send()

        @pl.when(z != mid)
        def _():
            up(s).wait_send()

        @pl.when(jnp.logical_and(z <= mid, has_l))
        def _():
            final_down(s).wait_send()

        @pl.when(jnp.logical_and(z >= mid, has_r))
        def _():
            final_up(s).wait_send()

        share(s).wait_send()

    loop(0, half, drain)
    total = sqs[0]
    for d in range(1, nc):
        sends[d - 1].wait_recv()
        total = total + sqs[d]
    for c in sends:
        c.wait_send()
    for i in range(2 * half):
        sq[i] = jnp.broadcast_to(total[:, i : i + 1], (8, 128))


def right_total(part, nr, nc):
    cols = part.shape[1]
    n = RANK // 8
    half = n // 2
    vm = pl.BlockSpec(memory_space=VMEM)
    piece = VMEM((half, 8, cols), F32)
    out, sq = pl.pallas_call(
        functools.partial(total_kernel, nr, nc),
        in_specs=[vm],
        out_specs=[vm, vm],
        out_shape=[
            jax.ShapeDtypeStruct((n, 8, cols), F32),
            jax.ShapeDtypeStruct((n, 8, 128), F32),
        ],
        scratch_shapes=[piece, piece, piece, piece, VMEM((nc, 8, 128), F32)]
        + [DMA((half,))] * 10
        + [DMA((nc - 1,))] * 2,
        compiler_params=pltpu.CompilerParams(
            collective_id=1, has_side_effects=True, vmem_limit_bytes=LIMIT
        ),
    )(part.reshape(n, 8, cols))
    return out.reshape(RANK, cols), sq.reshape(RANK, 128)


def final_kernel(scale, g_ref, m_ref, w_ref, hi_ref, lo_ref, rt_ref, sq_ref, nw_ref, nm_ref, nf_ref):
    rt = rt_ref[...]
    hi = hi_ref[...]
    ft = rt / jnp.sqrt(sq_ref[:, :1] / COLS + 1e-06)
    nf_ref[...] = ft.T
    buffer = g_ref[...].astype(F32) + m_ref[...].astype(F32)
    nm_ref[...] = (buffer - (1.0 - decay) * mm(hi, rt.astype(BF16))).astype(BF16)
    f_hi, f_lo = split(ft)
    update = mm(hi, f_hi) + mm(lo_ref[...], f_hi) + mm(hi, f_lo)
    nw_ref[...] = (w_ref[...].astype(F32) - scale * update).astype(BF16)


def final(g, m, w, hi, lo, rt, sq):
    rows, cols = g.shape
    tile = tile_of(cols)
    block = pl.BlockSpec((rows, tile), lambda i: (0, i))
    return pl.pallas_call(
        functools.partial(final_kernel, step_size * (ROWS / RANK) ** 0.5),
        grid=(cols // tile,),
        in_specs=[
            block,
            block,
            block,
            whole((rows, RANK)),
            whole((rows, RANK)),
            pl.BlockSpec((RANK, tile), lambda i: (0, i)),
            whole((RANK, 128)),
        ],
        out_specs=[block, block, pl.BlockSpec((tile, RANK), lambda i: (i, 0))],
        out_shape=[
            jax.ShapeDtypeStruct((rows, cols), BF16),
            jax.ShapeDtypeStruct((rows, cols), BF16),
            jax.ShapeDtypeStruct((cols, RANK), F32),
        ],
        compiler_params=pltpu.CompilerParams(vmem_limit_bytes=LIMIT),
    )(g, m, w, hi, lo, rt, sq)


def local(nr, nc, gradient, momentum, weight, right_factor):
    part = left_part(gradient, momentum, right_factor)
    left, gram = sums(part, nr, nc)
    hi, lo, t = ortho_of(gram, left)
    rt, sq = right_total(right_part(gradient, momentum, t), nr, nc)
    return tuple(final(gradient, momentum, weight, hi, lo, rt, sq))


def solution(mesh):
    in_specs = (P("row", "col"), P("row", "col"), P("row", "col"), P("col", None))
    out_specs = (P("row", "col"), P("row", "col"), P("col", None))
    body = functools.partial(local, mesh.shape["row"], mesh.shape["col"])
    return jax.shard_map(body, mesh=mesh, in_specs=in_specs, out_specs=out_specs, check_vma=False)
```

```python
import functools

import jax
import jax.numpy as jnp
from jax import lax
from jax.experimental import pallas as pl
from jax.experimental.pallas import tpu as pltpu
from jax.sharding import PartitionSpec as P

ROWS = 8192
COLS = 26624
RANK = 256

decay = 0.95
step_size = 0.3

MESH = pl.DeviceIdType.MESH
HIGH = lax.Precision.HIGHEST
F32 = jnp.float32
BF16 = jnp.bfloat16
VMEM = pltpu.VMEM
DMA = pltpu.SemaphoreType.DMA
LIMIT = 56 * 1024 * 1024


def split(x):
    hi = x.astype(BF16)
    return hi, (x - hi.astype(F32)).astype(BF16)


def mm(a, b):
    return jnp.dot(a, b, preferred_element_type=F32)


def tile_of(cols):
    for tile in (512, 256, 128):
        if cols % tile == 0:
            return tile
    return cols


def whole(shape):
    return pl.BlockSpec(shape, lambda i: (0,) * len(shape))


def left_kernel(g_ref, m_ref, r_ref, out_ref):
    @pl.when(pl.program_id(0) == 0)
    def _():
        out_ref[...] = jnp.zeros_like(out_ref)

    g, m = g_ref[...], m_ref[...]
    r_hi, r_lo = split(r_ref[...])
    out_ref[...] += mm(jnp.concatenate([g, m, g, m], axis=1), jnp.concatenate([r_hi, r_hi, r_lo, r_lo], axis=0))


def left_part(g, m, r):
    rows, cols = g.shape
    tile = tile_of(cols)
    return pl.pallas_call(
        left_kernel,
        grid=(cols // tile,),
        in_specs=[
            pl.BlockSpec((rows, tile), lambda i: (0, i)),
            pl.BlockSpec((rows, tile), lambda i: (0, i)),
            pl.BlockSpec((tile, RANK), lambda i: (i, 0)),
        ],
        out_specs=whole((rows, RANK)),
        out_shape=jax.ShapeDtypeStruct((rows, RANK), F32),
        compiler_params=pltpu.CompilerParams(vmem_limit_bytes=LIMIT),
    )(g, m, r)


def greet(peers):
    barrier = pltpu.get_barrier_semaphore()
    for peer in peers:
        pl.semaphore_signal(barrier, inc=1, device_id=peer, device_id_type=MESH)
    return barrier


def sums_kernel(nr, nc, part, left, gram, l_in, g_part, g_in, ls, lr, las, lar, gs, gr, gas, gar):
    ri, ci = lax.axis_index("row"), lax.axis_index("col")
    cols = [lax.rem(ci + d, nc) for d in range(nc)]
    rows = [lax.rem(ri + d, nr) for d in range(nr)]
    barrier = greet([{"col": p} for p in cols[1:]] + [{"row": p} for p in rows[1:]])
    pl.semaphore_wait(barrier, nc + nr - 2)

    def copy(src, dst, send, recv, peer):
        return pltpu.make_async_remote_copy(
            src_ref=src, dst_ref=dst, send_sem=send, recv_sem=recv, device_id=peer, device_id_type=MESH
        )

    def reduce_gather(axis, n, me, others, src, slots, total, s1, r1, s2, r2):
        first = [
            copy(src.at[others[d]], slots.at[d - 1], s1.at[d - 1], r1.at[d - 1], {axis: others[d]})
            for d in range(1, n)
        ]
        for c in first:
            c.start()
        acc = src[me]
        for d in range(1, n):
            first[d - 1].wait_recv()
            acc = acc + slots[d - 1]
        total[me] = acc
        second = [
            copy(total.at[me], total.at[me], s2.at[d - 1], r2.at[d - 1], {axis: others[d]})
            for d in range(1, n)
        ]
        for c in second:
            c.start()
        for d in range(1, n):
            owner = lax.rem(me + n - d, n)
            copy(total.at[owner], total.at[owner], s2.at[d - 1], r2.at[d - 1], {axis: others[d]}).wait_recv()
        for c in first + second:
            c.wait_send()

    reduce_gather("col", nc, ci, cols, part, l_in, left, ls, lr, las, lar)
    total = jnp.zeros((RANK, RANK), F32)
    for k in range(nc):
        block = left[k]
        total += jnp.dot(block.T, block, precision=HIGH, preferred_element_type=F32)
    g_part[...] = total.reshape(g_part.shape)
    reduce_gather("row", nr, ri, rows, g_part, g_in, gram, gs, gr, gas, gar)


def sums(part, nr, nc):
    rows = part.shape[0]
    piece, gpiece = rows // nc, RANK // nr
    vm = pl.BlockSpec(memory_space=VMEM)
    left, gram = pl.pallas_call(
        functools.partial(sums_kernel, nr, nc),
        in_specs=[vm],
        out_specs=[vm, vm],
        out_shape=[
            jax.ShapeDtypeStruct((nc, piece, RANK), F32),
            jax.ShapeDtypeStruct((nr, gpiece, RANK), F32),
        ],
        scratch_shapes=[
            VMEM((nc - 1, piece, RANK), F32),
            VMEM((nr, gpiece, RANK), F32),
            VMEM((nr - 1, gpiece, RANK), F32),
        ]
        + [DMA((nc - 1,))] * 4
        + [DMA((nr - 1,))] * 4,
        compiler_params=pltpu.CompilerParams(
            collective_id=0, has_side_effects=True, vmem_limit_bytes=LIMIT
        ),
    )(part.reshape(nc, piece, RANK))
    return left.reshape(rows, RANK), gram.reshape(RANK, RANK)


def ortho_kernel(gram_ref, left_ref, o_ref, t_ref, work, inv):
    nb, group = 32, 8
    gram = gram_ref[...]
    eye = lax.broadcasted_iota(jnp.int32, (RANK, RANK), 0) == lax.broadcasted_iota(
        jnp.int32, (RANK, RANK), 1
    )
    trace = jnp.sum(jnp.sum(jnp.where(eye, gram, 0.0), axis=1, keepdims=True), axis=0, keepdims=True)
    work[:, :RANK] = gram + jnp.where(eye, 1e-06 * trace / RANK, 0.0)
    work[:, RANK:] = eye.astype(F32)
    inv[...] = jnp.zeros_like(inv)
    for r0 in range(0, RANK, nb):
        lo = 0 if r0 < 128 else 128
        width = 384
        panel = work[r0 : r0 + nb, lo : lo + width]
        row_id = lax.broadcasted_iota(jnp.int32, (nb, 128), 0)
        for j0 in range(0, nb, group):
            p = r0 + j0 - lo
            column = [
                jnp.broadcast_to(panel[:, p + k : p + k + 1], (nb, 128)) for k in range(group)
            ]
            for k in range(group):
                j = j0 + k
                factor = column[k] * (1.0 / column[k][j : j + 1, :])
                factor = jnp.where(row_id > j, factor, 0.0)
                for q in range(k + 1, group):
                    column[q] = column[q] - factor * column[q][j : j + 1, :]
                panel = panel - jnp.concatenate([factor] * (width // 128), axis=1) * panel[j : j + 1, :]
        lane = lax.broadcasted_iota(jnp.int32, (nb, width), 1)
        sub = lax.broadcasted_iota(jnp.int32, (nb, width), 0)
        pivots = jnp.sum(jnp.where(lane == sub + (r0 - lo), panel, 0.0), axis=1, keepdims=True)
        panel = panel / jnp.sqrt(pivots)
        inv[r0 : r0 + nb, 0 : lo + width - RANK] = panel[:, RANK - lo :]
        if r0 + nb < RANK:
            mult = panel[:, : RANK - lo].T
            mult = mult[r0 + nb - lo :, :]
            work[r0 + nb :, lo : lo + width] -= jnp.dot(
                mult, panel, precision=HIGH, preferred_element_type=F32
            )
    ortho = lax.dot_general(
        left_ref[...], inv[...], (((1,), (1,)), ((), ())), precision=HIGH, preferred_element_type=F32
    )
    hi, low = split(ortho)
    o_ref[...] = jnp.concatenate([hi, low, hi], axis=1)
    hi, low = split(ortho.T)
    t_ref[:RANK, :] = hi
    t_ref[RANK:, :] = low


def ortho_of(gram, left):
    rows = left.shape[0]
    vm = pl.BlockSpec(memory_space=VMEM)
    return pl.pallas_call(
        ortho_kernel,
        in_specs=[vm, vm],
        out_specs=[vm, vm],
        out_shape=[
            jax.ShapeDtypeStruct((rows, 3 * RANK), BF16),
            jax.ShapeDtypeStruct((2 * RANK, rows), BF16),
        ],
        scratch_shapes=[VMEM((RANK, 2 * RANK), F32), VMEM((RANK, RANK), F32)],
        compiler_params=pltpu.CompilerParams(vmem_limit_bytes=LIMIT),
    )(gram, left)


def right_kernel(g_ref, m_ref, t_ref, out_ref):
    t = t_ref[...]
    both = mm(jnp.concatenate([t, t], axis=1), jnp.concatenate([g_ref[...], m_ref[...]], axis=0))
    out_ref[...] = both[:RANK] + both[RANK:]


def right_part(g, m, t):
    rows, cols = g.shape
    tile = tile_of(cols)
    return pl.pallas_call(
        right_kernel,
        grid=(cols // tile,),
        in_specs=[
            pl.BlockSpec((rows, tile), lambda i: (0, i)),
            pl.BlockSpec((rows, tile), lambda i: (0, i)),
            whole((2 * RANK, rows)),
        ],
        out_specs=pl.BlockSpec((RANK, tile), lambda i: (0, i)),
        out_shape=jax.ShapeDtypeStruct((RANK, cols), F32),
        compiler_params=pltpu.CompilerParams(vmem_limit_bytes=LIMIT),
    )(g, m, t)


def total_kernel(nr, nc, x, out, sq, c_in, l_in, r_in, acc, sqs, cs, cr, rs, lr, rr, fl, fr, fz, ps, pr, ss, sr):
    nz = nr // 2
    half = x.shape[0] // 2
    ri, ci = lax.axis_index("row"), lax.axis_index("col")
    z, core = ri // 2, lax.rem(ri, 2)
    partner = ri + 1 - 2 * core
    mine, theirs = core * half, (1 - core) * half
    lower, upper = jnp.maximum(ri - 2, core), jnp.minimum(ri + 2, nr - 2 + core)
    cols = [lax.rem(ci + d, nc) for d in range(nc)]
    has_l, has_r = z > 0, z < nz - 1

    barrier = greet([{"row": partner}] + [{"col": p} for p in cols[1:]])

    @pl.when(has_l)
    def _():
        pl.semaphore_signal(barrier, inc=1, device_id={"row": lower}, device_id_type=MESH)

    @pl.when(has_r)
    def _():
        pl.semaphore_signal(barrier, inc=1, device_id={"row": upper}, device_id_type=MESH)

    pl.semaphore_wait(barrier, nc + jnp.minimum(z, 1) + jnp.minimum(nz - 1 - z, 1))

    def copy(src, dst, send, recv, peer, axis="row"):
        return pltpu.make_async_remote_copy(
            src_ref=src, dst_ref=dst, send_sem=send, recv_sem=recv, device_id={axis: peer}, device_id_type=MESH
        )

    def core_copy(s):
        return copy(x.at[theirs + s], c_in.at[s], cs.at[s], cr.at[s], partner)

    def up(s):
        return copy(acc.at[s], l_in.at[s], rs.at[s], lr.at[s], upper)

    def down(s):
        return copy(acc.at[s], r_in.at[s], rs.at[s], rr.at[s], lower)

    def final_down(s):
        return copy(out.at[mine + s], out.at[mine + s], fl.at[s], fz.at[s], lower)

    def final_up(s):
        return copy(out.at[mine + s], out.at[mine + s], fr.at[s], fz.at[s], upper)

    def share(s):
        return copy(out.at[mine + s], out.at[mine + s], ps.at[s], pr.at[s], partner)

    def share_in(s):
        return copy(out.at[theirs + s], out.at[theirs + s], ps.at[s], pr.at[s], partner)

    def centre(s):
        return nz // 2 - 1 + lax.rem(s + core, 2)

    def from_lower(s):
        @pl.when(has_l)
        def _():
            up(s).wait_recv()
            acc[s] += l_in[s]

    def from_upper(s):
        @pl.when(has_r)
        def _():
            down(s).wait_recv()
            acc[s] += r_in[s]

    def reduce(s):
        mid = centre(s)
        core_copy(s).wait_recv()
        acc[s] = x[mine + s] + c_in[s]

        @pl.when(z < mid)
        def _():
            from_lower(s)
            up(s).start()

        @pl.when(z > mid)
        def _():
            from_upper(s)
            down(s).start()

        @pl.when(z == mid)
        def _():
            from_lower(s)
            from_upper(s)
            out[mine + s] = acc[s]

            @pl.when(has_l)
            def _():
                final_down(s).start()

            @pl.when(has_r)
            def _():
                final_up(s).start()

            share(s).start()

    def spread(s):
        mid = centre(s)

        @pl.when(z < mid)
        def _():
            final_down(s).wait_recv()

            @pl.when(has_l)
            def _():
                final_down(s).start()

            share(s).start()

        @pl.when(z > mid)
        def _():
            final_up(s).wait_recv()

            @pl.when(has_r)
            def _():
                final_up(s).start()

            share(s).start()

    def loop(lo, hi, body):
        def step(s, carry):
            body(s)
            return carry

        lax.fori_loop(lo, hi, step, 0)

    loop(0, half, lambda s: core_copy(s).start())

    end = jnp.logical_or(z == 0, z == nz - 1)

    if nz > 2:

        @pl.when(end)
        def _():
            loop(0, half, reduce)
            loop(0, half, spread)

        @pl.when(jnp.logical_not(end))
        def _():
            loop(0, 2, reduce)

            def both(t):
                reduce(t)
                spread(t - 2)

            loop(2, half, both)
            loop(half - 2, half, spread)

    else:
        loop(0, half, reduce)
        loop(0, half, spread)

    lane = lax.broadcasted_iota(jnp.int32, (8, 128), 1)

    def square(i, carry):
        v = out[i]
        return carry + jnp.where(lane == i, jnp.sum(v * v, axis=1, keepdims=True), 0.0)

    def own(s, carry):
        return square(mine + s, carry)

    def other(s, carry):
        share_in(s).wait_recv()
        return square(theirs + s, carry)

    carry = lax.fori_loop(0, half, own, jnp.zeros((8, 128), F32))
    sqs[0] = lax.fori_loop(0, half, other, carry)
    sends = [copy(sqs.at[0], sqs.at[d], ss.at[d - 1], sr.at[d - 1], cols[d], "col") for d in range(1, nc)]
    for c in sends:
        c.start()

    def drain(s):
        mid = centre(s)
        core_copy(s).wait_send()

        @pl.when(z != mid)
        def _():
            up(s).wait_send()

        @pl.when(jnp.logical_and(z <= mid, has_l))
        def _():
            final_down(s).wait_send()

        @pl.when(jnp.logical_and(z >= mid, has_r))
        def _():
            final_up(s).wait_send()

        share(s).wait_send()

    loop(0, half, drain)
    total = sqs[0]
    for d in range(1, nc):
        sends[d - 1].wait_recv()
        total = total + sqs[d]
    for c in sends:
        c.wait_send()
    for i in range(2 * half):
        sq[i] = jnp.broadcast_to(total[:, i : i + 1], (8, 128))


def right_total(part, nr, nc):
    cols = part.shape[1]
    n = RANK // 8
    half = n // 2
    vm = pl.BlockSpec(memory_space=VMEM)
    piece = VMEM((half, 8, cols), F32)
    out, sq = pl.pallas_call(
        functools.partial(total_kernel, nr, nc),
        in_specs=[vm],
        out_specs=[vm, vm],
        out_shape=[
            jax.ShapeDtypeStruct((n, 8, cols), F32),
            jax.ShapeDtypeStruct((n, 8, 128), F32),
        ],
        scratch_shapes=[piece, piece, piece, piece, VMEM((nc, 8, 128), F32)]
        + [DMA((half,))] * 10
        + [DMA((nc - 1,))] * 2,
        compiler_params=pltpu.CompilerParams(
            collective_id=1, has_side_effects=True, vmem_limit_bytes=LIMIT
        ),
    )(part.reshape(n, 8, cols))
    return out.reshape(RANK, cols), sq.reshape(RANK, 128)


def final_kernel(scale, g_ref, m_ref, w_ref, o_ref, rt_ref, sq_ref, nw_ref, nm_ref, nf_ref):
    rt = rt_ref[...]
    ft = rt / jnp.sqrt(sq_ref[:, :1] / COLS + 1e-06)
    nf_ref[...] = ft.T
    buffer = g_ref[...].astype(F32) + m_ref[...].astype(F32)
    nm_ref[...] = (buffer - mm(o_ref[:, :RANK], ((1.0 - decay) * rt).astype(BF16))).astype(BF16)
    f_hi, f_lo = split(scale * ft)
    update = mm(o_ref[...], jnp.concatenate([f_hi, f_hi, f_lo], axis=0))
    nw_ref[...] = (w_ref[...].astype(F32) - update).astype(BF16)


def final(g, m, w, o, rt, sq):
    rows, cols = g.shape
    tile = tile_of(cols)
    block = pl.BlockSpec((rows, tile), lambda i: (0, i))
    return pl.pallas_call(
        functools.partial(final_kernel, step_size * (ROWS / RANK) ** 0.5),
        grid=(cols // tile,),
        in_specs=[
            block,
            block,
            block,
            whole((rows, 3 * RANK)),
            pl.BlockSpec((RANK, tile), lambda i: (0, i)),
            whole((RANK, 128)),
        ],
        out_specs=[block, block, pl.BlockSpec((tile, RANK), lambda i: (i, 0))],
        out_shape=[
            jax.ShapeDtypeStruct((rows, cols), BF16),
            jax.ShapeDtypeStruct((rows, cols), BF16),
            jax.ShapeDtypeStruct((cols, RANK), F32),
        ],
        compiler_params=pltpu.CompilerParams(vmem_limit_bytes=LIMIT),
    )(g, m, w, o, rt, sq)


def local(nr, nc, gradient, momentum, weight, right_factor):
    part = left_part(gradient, momentum, right_factor)
    left, gram = sums(part, nr, nc)
    o, t = ortho_of(gram, left)
    rt, sq = right_total(right_part(gradient, momentum, t), nr, nc)
    return tuple(final(gradient, momentum, weight, o, rt, sq))


def solution(mesh):
    in_specs = (P("row", "col"), P("row", "col"), P("row", "col"), P("col", None))
    out_specs = (P("row", "col"), P("row", "col"), P("col", None))
    body = functools.partial(local, mesh.shape["row"], mesh.shape["col"])
    return jax.shard_map(body, mesh=mesh, in_specs=in_specs, out_specs=out_specs, check_vma=False)
```

```python
import functools

import jax
import jax.numpy as jnp
from jax import lax
from jax.experimental import pallas as pl
from jax.experimental.pallas import tpu as pltpu
from jax.sharding import PartitionSpec as P

ROWS = 8192
COLS = 26624
RANK = 256

decay = 0.95
step_size = 0.3

MESH = pl.DeviceIdType.MESH
HIGH = lax.Precision.HIGHEST
F32 = jnp.float32
BF16 = jnp.bfloat16
VMEM = pltpu.VMEM
DMA = pltpu.SemaphoreType.DMA
LIMIT = 56 * 1024 * 1024


def split(x):
    hi = x.astype(BF16)
    return hi, (x - hi.astype(F32)).astype(BF16)


def mm(a, b):
    return jnp.dot(a, b, preferred_element_type=F32)


def tile_of(cols):
    for tile in (512, 256, 128):
        if cols % tile == 0:
            return tile
    return cols


def whole(shape):
    return pl.BlockSpec(shape, lambda i: (0,) * len(shape))


def left_kernel(g_ref, m_ref, r_ref, out_ref):
    @pl.when(pl.program_id(0) == 0)
    def _():
        out_ref[...] = jnp.zeros_like(out_ref)

    g, m = g_ref[...], m_ref[...]
    r_hi, r_lo = split(r_ref[...])
    out_ref[...] += mm(jnp.concatenate([g, m, g, m], axis=1), jnp.concatenate([r_hi, r_hi, r_lo, r_lo], axis=0))


def left_part(g, m, r):
    rows, cols = g.shape
    tile = tile_of(cols)
    return pl.pallas_call(
        left_kernel,
        grid=(cols // tile,),
        in_specs=[
            pl.BlockSpec((rows, tile), lambda i: (0, i)),
            pl.BlockSpec((rows, tile), lambda i: (0, i)),
            pl.BlockSpec((tile, RANK), lambda i: (i, 0)),
        ],
        out_specs=whole((rows, RANK)),
        out_shape=jax.ShapeDtypeStruct((rows, RANK), F32),
        compiler_params=pltpu.CompilerParams(vmem_limit_bytes=LIMIT),
    )(g, m, r)


def greet(peers):
    barrier = pltpu.get_barrier_semaphore()
    for peer in peers:
        pl.semaphore_signal(barrier, inc=1, device_id=peer, device_id_type=MESH)
    return barrier


def sums_kernel(nr, nc, part, left, gram, l_in, g_part, g_in, ls, lr, las, lar, gs, gr, gas, gar):
    ri, ci = lax.axis_index("row"), lax.axis_index("col")
    cols = [lax.rem(ci + d, nc) for d in range(nc)]
    rows = [lax.rem(ri + d, nr) for d in range(nr)]
    barrier = greet([{"col": p} for p in cols[1:]] + [{"row": p} for p in rows[1:]])
    pl.semaphore_wait(barrier, nc + nr - 2)

    def copy(src, dst, send, recv, peer):
        return pltpu.make_async_remote_copy(
            src_ref=src, dst_ref=dst, send_sem=send, recv_sem=recv, device_id=peer, device_id_type=MESH
        )

    def reduce_gather(axis, n, me, others, src, slots, total, s1, r1, s2, r2):
        first = [
            copy(src.at[others[d]], slots.at[d - 1], s1.at[d - 1], r1.at[d - 1], {axis: others[d]})
            for d in range(1, n)
        ]
        for c in first:
            c.start()
        acc = src[me]
        for d in range(1, n):
            first[d - 1].wait_recv()
            acc = acc + slots[d - 1]
        total[me] = acc
        second = [
            copy(total.at[me], total.at[me], s2.at[d - 1], r2.at[d - 1], {axis: others[d]})
            for d in range(1, n)
        ]
        for c in second:
            c.start()
        for d in range(1, n):
            owner = lax.rem(me + n - d, n)
            copy(total.at[owner], total.at[owner], s2.at[d - 1], r2.at[d - 1], {axis: others[d]}).wait_recv()
        for c in first + second:
            c.wait_send()

    reduce_gather("col", nc, ci, cols, part, l_in, left, ls, lr, las, lar)
    total = jnp.zeros((RANK, RANK), F32)
    for k in range(nc):
        block = left[k]
        total += jnp.dot(block.T, block, precision=HIGH, preferred_element_type=F32)
    g_part[...] = total.reshape(g_part.shape)
    reduce_gather("row", nr, ri, rows, g_part, g_in, gram, gs, gr, gas, gar)


def sums(part, nr, nc):
    rows = part.shape[0]
    piece, gpiece = rows // nc, RANK // nr
    vm = pl.BlockSpec(memory_space=VMEM)
    left, gram = pl.pallas_call(
        functools.partial(sums_kernel, nr, nc),
        in_specs=[vm],
        out_specs=[vm, vm],
        out_shape=[
            jax.ShapeDtypeStruct((nc, piece, RANK), F32),
            jax.ShapeDtypeStruct((nr, gpiece, RANK), F32),
        ],
        scratch_shapes=[
            VMEM((nc - 1, piece, RANK), F32),
            VMEM((nr, gpiece, RANK), F32),
            VMEM((nr - 1, gpiece, RANK), F32),
        ]
        + [DMA((nc - 1,))] * 4
        + [DMA((nr - 1,))] * 4,
        compiler_params=pltpu.CompilerParams(
            collective_id=0, has_side_effects=True, vmem_limit_bytes=LIMIT
        ),
    )(part.reshape(nc, piece, RANK))
    return left.reshape(rows, RANK), gram.reshape(RANK, RANK)


def ortho_kernel(gram_ref, left_ref, o_ref, t_ref, work, inv):
    nb, group = 32, 8
    gram = gram_ref[...]
    eye = lax.broadcasted_iota(jnp.int32, (RANK, RANK), 0) == lax.broadcasted_iota(
        jnp.int32, (RANK, RANK), 1
    )
    trace = jnp.sum(jnp.sum(jnp.where(eye, gram, 0.0), axis=1, keepdims=True), axis=0, keepdims=True)
    work[:, :RANK] = gram + jnp.where(eye, 1e-06 * trace / RANK, 0.0)
    work[:, RANK:] = eye.astype(F32)
    inv[...] = jnp.zeros_like(inv)
    for r0 in range(0, RANK, nb):
        lo = 0 if r0 < 128 else 128
        width = 384
        panel = work[r0 : r0 + nb, lo : lo + width]
        row_id = lax.broadcasted_iota(jnp.int32, (nb, 128), 0)
        for j0 in range(0, nb, group):
            p = r0 + j0 - lo
            column = [
                jnp.broadcast_to(panel[:, p + k : p + k + 1], (nb, 128)) for k in range(group)
            ]
            for k in range(group):
                j = j0 + k
                factor = column[k] * (1.0 / column[k][j : j + 1, :])
                factor = jnp.where(row_id > j, factor, 0.0)
                for q in range(k + 1, group):
                    column[q] = column[q] - factor * column[q][j : j + 1, :]
                panel = panel - jnp.concatenate([factor] * (width // 128), axis=1) * panel[j : j + 1, :]
        lane = lax.broadcasted_iota(jnp.int32, (nb, width), 1)
        sub = lax.broadcasted_iota(jnp.int32, (nb, width), 0)
        pivots = jnp.sum(jnp.where(lane == sub + (r0 - lo), panel, 0.0), axis=1, keepdims=True)
        panel = panel / jnp.sqrt(pivots)
        inv[r0 : r0 + nb, 0 : lo + width - RANK] = panel[:, RANK - lo :]
        if r0 + nb < RANK:
            mult = panel[:, : RANK - lo].T
            mult = mult[r0 + nb - lo :, :]
            work[r0 + nb :, lo : lo + width] -= jnp.dot(
                mult, panel, precision=HIGH, preferred_element_type=F32
            )
    ortho = lax.dot_general(
        left_ref[...], inv[...], (((1,), (1,)), ((), ())), precision=HIGH, preferred_element_type=F32
    )
    hi, low = split(ortho)
    o_ref[...] = jnp.concatenate([hi, low, hi], axis=1)
    hi, low = split(ortho.T)
    t_ref[:RANK, :] = hi
    t_ref[RANK:, :] = low


def ortho_of(gram, left):
    rows = left.shape[0]
    vm = pl.BlockSpec(memory_space=VMEM)
    return pl.pallas_call(
        ortho_kernel,
        in_specs=[vm, vm],
        out_specs=[vm, vm],
        out_shape=[
            jax.ShapeDtypeStruct((rows, 3 * RANK), BF16),
            jax.ShapeDtypeStruct((2 * RANK, rows), BF16),
        ],
        scratch_shapes=[VMEM((RANK, 2 * RANK), F32), VMEM((RANK, RANK), F32)],
        compiler_params=pltpu.CompilerParams(vmem_limit_bytes=LIMIT),
    )(gram, left)


def right_kernel(nr, nc, g, m, t_ref, out, sq, g_buf, m_buf, x, c_in, l_in, r_in, acc, sqs, gs, ms, cs, cr, rs, lr, rr, fl, fr, fz, ps, pr, ss, sr):
    nz = nr // 2
    n, tile = x.shape[0], x.shape[3]
    ri, ci = lax.axis_index("row"), lax.axis_index("col")
    z, core = ri // 2, lax.rem(ri, 2)
    other = 1 - core
    partner = ri + 1 - 2 * core
    lower, upper = jnp.maximum(ri - 2, core), jnp.minimum(ri + 2, nr - 2 + core)
    cols = [lax.rem(ci + d, nc) for d in range(nc)]
    has_l, has_r = z > 0, z < nz - 1

    def fetch(s):
        at = pl.ds(pl.multiple_of(s * tile, tile), tile)
        slot = lax.rem(s, 2)
        return (
            pltpu.make_async_copy(g.at[:, at], g_buf.at[slot], gs.at[slot]),
            pltpu.make_async_copy(m.at[:, at], m_buf.at[slot], ms.at[slot]),
        )

    for s in range(min(2, n)):
        for c in fetch(s):
            c.start()

    barrier = greet([{"row": partner}] + [{"col": p} for p in cols[1:]])

    @pl.when(has_l)
    def _():
        pl.semaphore_signal(barrier, inc=1, device_id={"row": lower}, device_id_type=MESH)

    @pl.when(has_r)
    def _():
        pl.semaphore_signal(barrier, inc=1, device_id={"row": upper}, device_id_type=MESH)

    pl.semaphore_wait(barrier, nc + jnp.minimum(z, 1) + jnp.minimum(nz - 1 - z, 1))

    def copy(src, dst, send, recv, peer, axis="row"):
        return pltpu.make_async_remote_copy(
            src_ref=src, dst_ref=dst, send_sem=send, recv_sem=recv, device_id={axis: peer}, device_id_type=MESH
        )

    def core_copy(s):
        return copy(x.at[s, other], c_in.at[s], cs.at[s], cr.at[s], partner)

    def up(s):
        return copy(acc.at[s], l_in.at[s], rs.at[s], lr.at[s], upper)

    def down(s):
        return copy(acc.at[s], r_in.at[s], rs.at[s], rr.at[s], lower)

    def final_down(s):
        return copy(out.at[s, core], out.at[s, core], fl.at[s], fz.at[s], lower)

    def final_up(s):
        return copy(out.at[s, core], out.at[s, core], fr.at[s], fz.at[s], upper)

    def share(s):
        return copy(out.at[s, core], out.at[s, core], ps.at[s], pr.at[s], partner)

    def share_in(s):
        return copy(out.at[s, other], out.at[s, other], ps.at[s], pr.at[s], partner)

    def centre(s):
        return nz // 2 - 1 + lax.rem(s + core, 2)

    def product(s):
        slot = lax.rem(s, 2)
        for c in fetch(s):
            c.wait()
        t = t_ref[...]
        both = mm(jnp.concatenate([t, t], axis=1), jnp.concatenate([g_buf[slot], m_buf[slot]], axis=0))
        x[s] = (both[:RANK] + both[RANK:]).reshape(2, RANK // 2, tile)
        core_copy(s).start()

        @pl.when(s + 2 < n)
        def _():
            for c in fetch(s + 2):
                c.start()

    def from_lower(s):
        @pl.when(has_l)
        def _():
            up(s).wait_recv()
            acc[s] += l_in[s]

    def from_upper(s):
        @pl.when(has_r)
        def _():
            down(s).wait_recv()
            acc[s] += r_in[s]

    def forward(s):
        mid = centre(s)
        core_copy(s).wait_recv()
        acc[s] = x[s, core] + c_in[s]

        @pl.when(z < mid)
        def _():
            from_lower(s)
            up(s).start()

        @pl.when(z > mid)
        def _():
            from_upper(s)
            down(s).start()

    def total(s):
        @pl.when(z == centre(s))
        def _():
            from_lower(s)
            from_upper(s)
            out[s, core] = acc[s]

            @pl.when(has_l)
            def _():
                final_down(s).start()

            @pl.when(has_r)
            def _():
                final_up(s).start()

            share(s).start()

    def spread(s):
        mid = centre(s)

        @pl.when(z < mid)
        def _():
            final_down(s).wait_recv()

            @pl.when(has_l)
            def _():
                final_down(s).start()

            share(s).start()

        @pl.when(z > mid)
        def _():
            final_up(s).wait_recv()

            @pl.when(has_r)
            def _():
                final_up(s).start()

            share(s).start()

    def loop(lo, hi, body):
        def step(s, carry):
            body(s)
            return carry

        lax.fori_loop(lo, hi, step, 0)

    def stages(lags):
        def body(i):
            for work, lag in lags:

                @pl.when(jnp.logical_and(i >= lag, i < n + lag))
                def _():
                    work(i - lag)

        loop(0, n + max(lag for _, lag in lags), body)

    if nz > 2:
        end = jnp.logical_or(z == 0, z == nz - 1)

        @pl.when(end)
        def _():
            stages([(product, 0), (forward, 2)])
            loop(0, n, spread)

        @pl.when(jnp.logical_not(end))
        def _():
            stages([(product, 0), (forward, 2), (total, 4), (spread, 6)])

    else:
        stages([(product, 0), (forward, 2), (total, 4), (spread, 6)])

    def drain(s):
        mid = centre(s)
        core_copy(s).wait_send()

        @pl.when(z != mid)
        def _():
            up(s).wait_send()

        @pl.when(jnp.logical_and(z <= mid, has_l))
        def _():
            final_down(s).wait_send()

        @pl.when(jnp.logical_and(z >= mid, has_r))
        def _():
            final_up(s).wait_send()

        share(s).wait_send()
        share_in(s).wait_recv()

    loop(0, n, drain)

    def square(s, carry):
        v = out[s].reshape(RANK, tile)
        for k in range(tile // 128):
            w = v[:, k * 128 : (k + 1) * 128]
            carry = carry + w * w
        return carry

    squares = lax.fori_loop(0, n, square, jnp.zeros((RANK, 128), F32))
    sqs[0] = jnp.broadcast_to(jnp.sum(squares.T, axis=0, keepdims=True), (8, RANK))
    sends = [copy(sqs.at[0], sqs.at[d], ss.at[d - 1], sr.at[d - 1], cols[d], "col") for d in range(1, nc)]
    for c in sends:
        c.start()
    total_sq = sqs[0]
    for d in range(1, nc):
        sends[d - 1].wait_recv()
        total_sq = total_sq + sqs[d]
    for c in sends:
        c.wait_send()
    sq[...] = total_sq


def right_total(g, m, t, nr, nc):
    rows, cols = g.shape
    tile = min(tile_of(cols), 256)
    n = cols // tile
    vm = pl.BlockSpec(memory_space=VMEM)
    hbm = pl.BlockSpec(memory_space=pl.ANY)
    piece = VMEM((n, RANK // 2, tile), F32)
    out, sq = pl.pallas_call(
        functools.partial(right_kernel, nr, nc),
        in_specs=[hbm, hbm, vm],
        out_specs=[vm, vm],
        out_shape=[
            jax.ShapeDtypeStruct((n, 2, RANK // 2, tile), F32),
            jax.ShapeDtypeStruct((8, RANK), F32),
        ],
        scratch_shapes=[
            VMEM((2, rows, tile), BF16),
            VMEM((2, rows, tile), BF16),
            VMEM((n, 2, RANK // 2, tile), F32),
            piece,
            piece,
            piece,
            piece,
            VMEM((nc, 8, RANK), F32),
        ]
        + [DMA((2,))] * 2
        + [DMA((n,))] * 10
        + [DMA((nc - 1,))] * 2,
        compiler_params=pltpu.CompilerParams(
            collective_id=1, has_side_effects=True, vmem_limit_bytes=LIMIT
        ),
    )(g, m, t)
    return out.reshape(n, RANK, tile), sq


def final_kernel(scale, g_ref, m_ref, w_ref, o_ref, rt_ref, sq_ref, nw_ref, nm_ref, nf_ref):
    rt = jnp.concatenate([rt_ref[k] for k in range(rt_ref.shape[0])], axis=1)
    ft = rt / jnp.sqrt(sq_ref[...].T[:, :1] / COLS + 1e-06)
    nf_ref[...] = ft.T
    buffer = g_ref[...].astype(F32) + m_ref[...].astype(F32)
    nm_ref[...] = (buffer - mm(o_ref[:, :RANK], ((1.0 - decay) * rt).astype(BF16))).astype(BF16)
    f_hi, f_lo = split(scale * ft)
    update = mm(o_ref[...], jnp.concatenate([f_hi, f_hi, f_lo], axis=0))
    nw_ref[...] = (w_ref[...].astype(F32) - update).astype(BF16)


def final(g, m, w, o, rt, sq):
    rows, cols = g.shape
    tile = tile_of(cols)
    block = pl.BlockSpec((rows, tile), lambda i: (0, i))
    return pl.pallas_call(
        functools.partial(final_kernel, step_size * (ROWS / RANK) ** 0.5),
        grid=(cols // tile,),
        in_specs=[
            block,
            block,
            block,
            whole((rows, 3 * RANK)),
            pl.BlockSpec((tile // rt.shape[2], RANK, rt.shape[2]), lambda i: (i, 0, 0)),
            whole((8, RANK)),
        ],
        out_specs=[block, block, pl.BlockSpec((tile, RANK), lambda i: (i, 0))],
        out_shape=[
            jax.ShapeDtypeStruct((rows, cols), BF16),
            jax.ShapeDtypeStruct((rows, cols), BF16),
            jax.ShapeDtypeStruct((cols, RANK), F32),
        ],
        compiler_params=pltpu.CompilerParams(vmem_limit_bytes=LIMIT),
    )(g, m, w, o, rt, sq)


def local(nr, nc, gradient, momentum, weight, right_factor):
    part = left_part(gradient, momentum, right_factor)
    left, gram = sums(part, nr, nc)
    o, t = ortho_of(gram, left)
    rt, sq = right_total(gradient, momentum, t, nr, nc)
    return tuple(final(gradient, momentum, weight, o, rt, sq))


def solution(mesh):
    in_specs = (P("row", "col"), P("row", "col"), P("row", "col"), P("col", None))
    out_specs = (P("row", "col"), P("row", "col"), P("col", None))
    body = functools.partial(local, mesh.shape["row"], mesh.shape["col"])
    return jax.shard_map(body, mesh=mesh, in_specs=in_specs, out_specs=out_specs, check_vma=False)
```

```python
import functools

import jax
import jax.numpy as jnp
from jax import lax
from jax.experimental import pallas as pl
from jax.experimental.pallas import tpu as pltpu
from jax.sharding import PartitionSpec as P

ROWS = 8192
COLS = 26624
RANK = 256

decay = 0.95
step_size = 0.3

MESH = pl.DeviceIdType.MESH
HIGH = lax.Precision.HIGHEST
F32 = jnp.float32
BF16 = jnp.bfloat16
VMEM = pltpu.VMEM
DMA = pltpu.SemaphoreType.DMA
LIMIT = 56 * 1024 * 1024


def split(x):
    hi = x.astype(BF16)
    return hi, (x - hi.astype(F32)).astype(BF16)


def mm(a, b):
    return jnp.dot(a, b, preferred_element_type=F32)


def tile_of(cols):
    for tile in (512, 256, 128):
        if cols % tile == 0:
            return tile
    return cols


def whole(shape):
    return pl.BlockSpec(shape, lambda i: (0,) * len(shape))


def left_kernel(g_ref, m_ref, r_ref, out_ref):
    @pl.when(pl.program_id(0) == 0)
    def _():
        out_ref[...] = jnp.zeros_like(out_ref)

    g, m = g_ref[...], m_ref[...]
    r_hi, r_lo = split(r_ref[...])
    out_ref[...] += mm(jnp.concatenate([g, m, g, m], axis=1), jnp.concatenate([r_hi, r_hi, r_lo, r_lo], axis=0))


def left_part(g, m, r):
    rows, cols = g.shape
    tile = tile_of(cols)
    return pl.pallas_call(
        left_kernel,
        grid=(cols // tile,),
        in_specs=[
            pl.BlockSpec((rows, tile), lambda i: (0, i)),
            pl.BlockSpec((rows, tile), lambda i: (0, i)),
            pl.BlockSpec((tile, RANK), lambda i: (i, 0)),
        ],
        out_specs=whole((rows, RANK)),
        out_shape=jax.ShapeDtypeStruct((rows, RANK), F32),
        compiler_params=pltpu.CompilerParams(vmem_limit_bytes=LIMIT),
    )(g, m, r)


def greet(peers):
    barrier = pltpu.get_barrier_semaphore()
    for peer in peers:
        pl.semaphore_signal(barrier, inc=1, device_id=peer, device_id_type=MESH)
    return barrier


def sums_kernel(nr, nc, part, left, gram, l_in, g_part, g_in, g_col, ls, lr, las, lar, gcs, gcr, gs, gr, gas, gar):
    ri, ci = lax.axis_index("row"), lax.axis_index("col")
    cols = [lax.rem(ci + d, nc) for d in range(nc)]
    rows = [lax.rem(ri + d, nr) for d in range(nr)]
    barrier = greet([{"col": p} for p in cols[1:]] + [{"row": p} for p in rows[1:]])
    pl.semaphore_wait(barrier, nc + nr - 2)

    def copy(src, dst, send, recv, peer):
        return pltpu.make_async_remote_copy(
            src_ref=src, dst_ref=dst, send_sem=send, recv_sem=recv, device_id=peer, device_id_type=MESH
        )

    def scatter(axis, n, others, src, slots, send, recv):
        copies = [
            copy(src.at[others[d]], slots.at[d - 1], send.at[d - 1], recv.at[d - 1], {axis: others[d]})
            for d in range(1, n)
        ]
        for c in copies:
            c.start()
        return copies

    def gather(axis, n, me, others, total, send, recv):
        copies = [
            copy(total.at[me], total.at[me], send.at[d - 1], recv.at[d - 1], {axis: others[d]})
            for d in range(1, n)
        ]
        for c in copies:
            c.start()
        return copies

    def gathered(axis, n, me, others, total, send, recv):
        for d in range(1, n):
            owner = lax.rem(me + n - d, n)
            copy(total.at[owner], total.at[owner], send.at[d - 1], recv.at[d - 1], {axis: others[d]}).wait_recv()

    def added(acc, copies, slots):
        for d, c in enumerate(copies):
            c.wait_recv()
            acc = acc + slots[d]
        return acc

    sent = scatter("col", nc, cols, part, l_in, ls, lr)
    block = added(part[ci], sent, l_in)
    left[ci] = block
    sent += gather("col", nc, ci, cols, left, las, lar)
    product = jnp.dot(block.T, block, precision=HIGH, preferred_element_type=F32)
    g_part[...] = product.reshape(g_part.shape)
    over_row = scatter("row", nr, rows, g_part, g_in, gs, gr)
    g_col[0] = added(g_part[ri], over_row, g_in)
    over_col = [
        copy(g_col.at[0], g_col.at[d], gcs.at[d - 1], gcr.at[d - 1], {"col": cols[d]}) for d in range(1, nc)
    ]
    for c in over_col:
        c.start()
    piece = g_col[0]
    for d in range(1, nc):
        over_col[d - 1].wait_recv()
        piece = piece + g_col[d]
    gram[ri] = piece
    sent += over_row + over_col + gather("row", nr, ri, rows, gram, gas, gar)
    gathered("row", nr, ri, rows, gram, gas, gar)
    gathered("col", nc, ci, cols, left, las, lar)
    for c in sent:
        c.wait_send()


def sums(part, nr, nc):
    rows = part.shape[0]
    piece, gpiece = rows // nc, RANK // nr
    vm = pl.BlockSpec(memory_space=VMEM)
    left, gram = pl.pallas_call(
        functools.partial(sums_kernel, nr, nc),
        in_specs=[vm],
        out_specs=[vm, vm],
        out_shape=[
            jax.ShapeDtypeStruct((nc, piece, RANK), F32),
            jax.ShapeDtypeStruct((nr, gpiece, RANK), F32),
        ],
        scratch_shapes=[
            VMEM((nc - 1, piece, RANK), F32),
            VMEM((nr, gpiece, RANK), F32),
            VMEM((nr - 1, gpiece, RANK), F32),
            VMEM((nc, gpiece, RANK), F32),
        ]
        + [DMA((nc - 1,))] * 6
        + [DMA((nr - 1,))] * 4,
        compiler_params=pltpu.CompilerParams(
            collective_id=0, has_side_effects=True, vmem_limit_bytes=LIMIT
        ),
    )(part.reshape(nc, piece, RANK))
    return left.reshape(rows, RANK), gram.reshape(RANK, RANK)


def ortho_kernel(gram_ref, left_ref, o_ref, t_ref, work, inv):
    nb, group = 32, 8
    gram = gram_ref[...]
    eye = lax.broadcasted_iota(jnp.int32, (RANK, RANK), 0) == lax.broadcasted_iota(
        jnp.int32, (RANK, RANK), 1
    )
    trace = jnp.sum(jnp.sum(jnp.where(eye, gram, 0.0), axis=1, keepdims=True), axis=0, keepdims=True)
    work[:, :RANK] = gram + jnp.where(eye, 1e-06 * trace / RANK, 0.0)
    work[:, RANK:] = eye.astype(F32)
    inv[...] = jnp.zeros_like(inv)
    for r0 in range(0, RANK, nb):
        lo = 0 if r0 < 128 else 128
        width = 384
        panel = work[r0 : r0 + nb, lo : lo + width]
        row_id = lax.broadcasted_iota(jnp.int32, (nb, 128), 0)
        for j0 in range(0, nb, group):
            p = r0 + j0 - lo
            column = [
                jnp.broadcast_to(panel[:, p + k : p + k + 1], (nb, 128)) for k in range(group)
            ]
            for k in range(group):
                j = j0 + k
                factor = column[k] * (1.0 / column[k][j : j + 1, :])
                factor = jnp.where(row_id > j, factor, 0.0)
                for q in range(k + 1, group):
                    column[q] = column[q] - factor * column[q][j : j + 1, :]
                panel = panel - jnp.concatenate([factor] * (width // 128), axis=1) * panel[j : j + 1, :]
        lane = lax.broadcasted_iota(jnp.int32, (nb, width), 1)
        sub = lax.broadcasted_iota(jnp.int32, (nb, width), 0)
        pivots = jnp.sum(jnp.where(lane == sub + (r0 - lo), panel, 0.0), axis=1, keepdims=True)
        panel = panel / jnp.sqrt(pivots)
        inv[r0 : r0 + nb, 0 : lo + width - RANK] = panel[:, RANK - lo :]
        if r0 + nb < RANK:
            mult = panel[:, : RANK - lo].T
            mult = mult[r0 + nb - lo :, :]
            work[r0 + nb :, lo : lo + width] -= jnp.dot(
                mult, panel, precision=HIGH, preferred_element_type=F32
            )
    ortho = lax.dot_general(
        left_ref[...], inv[...], (((1,), (1,)), ((), ())), precision=HIGH, preferred_element_type=F32
    )
    hi, low = split(ortho)
    o_ref[...] = jnp.concatenate([hi, low, hi], axis=1)
    hi, low = split(ortho.T)
    t_ref[:RANK, :] = hi
    t_ref[RANK:, :] = low


def ortho_of(gram, left):
    rows = left.shape[0]
    vm = pl.BlockSpec(memory_space=VMEM)
    return pl.pallas_call(
        ortho_kernel,
        in_specs=[vm, vm],
        out_specs=[vm, vm],
        out_shape=[
            jax.ShapeDtypeStruct((rows, 3 * RANK), BF16),
            jax.ShapeDtypeStruct((2 * RANK, rows), BF16),
        ],
        scratch_shapes=[VMEM((RANK, 2 * RANK), F32), VMEM((RANK, RANK), F32)],
        compiler_params=pltpu.CompilerParams(vmem_limit_bytes=LIMIT),
    )(gram, left)


def right_kernel(nr, nc, g, m, t_ref, out, sq, g_buf, m_buf, x, c_in, l_in, r_in, acc, sqs, gs, ms, cs, cr, rs, lr, rr, fl, fr, fz, ps, pr, ss, sr):
    nz = nr // 2
    n, tile = x.shape[0], x.shape[3]
    ri, ci = lax.axis_index("row"), lax.axis_index("col")
    z, core = ri // 2, lax.rem(ri, 2)
    other = 1 - core
    partner = ri + 1 - 2 * core
    lower, upper = jnp.maximum(ri - 2, core), jnp.minimum(ri + 2, nr - 2 + core)
    cols = [lax.rem(ci + d, nc) for d in range(nc)]
    has_l, has_r = z > 0, z < nz - 1

    def fetch(s):
        at = pl.ds(pl.multiple_of(s * tile, tile), tile)
        slot = lax.rem(s, 2)
        return (
            pltpu.make_async_copy(g.at[:, at], g_buf.at[slot], gs.at[slot]),
            pltpu.make_async_copy(m.at[:, at], m_buf.at[slot], ms.at[slot]),
        )

    for s in range(min(2, n)):
        for c in fetch(s):
            c.start()

    barrier = greet([{"row": partner}] + [{"col": p} for p in cols[1:]])

    @pl.when(has_l)
    def _():
        pl.semaphore_signal(barrier, inc=1, device_id={"row": lower}, device_id_type=MESH)

    @pl.when(has_r)
    def _():
        pl.semaphore_signal(barrier, inc=1, device_id={"row": upper}, device_id_type=MESH)

    pl.semaphore_wait(barrier, nc + jnp.minimum(z, 1) + jnp.minimum(nz - 1 - z, 1))

    def copy(src, dst, send, recv, peer, axis="row"):
        return pltpu.make_async_remote_copy(
            src_ref=src, dst_ref=dst, send_sem=send, recv_sem=recv, device_id={axis: peer}, device_id_type=MESH
        )

    def core_copy(s):
        return copy(x.at[s, other], c_in.at[s], cs.at[s], cr.at[s], partner)

    def up(s):
        return copy(acc.at[s], l_in.at[s], rs.at[s], lr.at[s], upper)

    def down(s):
        return copy(acc.at[s], r_in.at[s], rs.at[s], rr.at[s], lower)

    def final_down(s):
        return copy(out.at[s, core], out.at[s, core], fl.at[s], fz.at[s], lower)

    def final_up(s):
        return copy(out.at[s, core], out.at[s, core], fr.at[s], fz.at[s], upper)

    def share(s):
        return copy(out.at[s, core], out.at[s, core], ps.at[s], pr.at[s], partner)

    def share_in(s):
        return copy(out.at[s, other], out.at[s, other], ps.at[s], pr.at[s], partner)

    def centre(s):
        return nz // 2 - 1 + lax.rem(s + core, 2)

    def product(s):
        slot = lax.rem(s, 2)
        for c in fetch(s):
            c.wait()
        t = t_ref[...]
        both = mm(jnp.concatenate([t, t], axis=1), jnp.concatenate([g_buf[slot], m_buf[slot]], axis=0))
        x[s] = (both[:RANK] + both[RANK:]).reshape(2, RANK // 2, tile)
        core_copy(s).start()

        @pl.when(s + 2 < n)
        def _():
            for c in fetch(s + 2):
                c.start()

    def from_lower(s):
        @pl.when(has_l)
        def _():
            up(s).wait_recv()
            acc[s] += l_in[s]

    def from_upper(s):
        @pl.when(has_r)
        def _():
            down(s).wait_recv()
            acc[s] += r_in[s]

    def forward(s):
        mid = centre(s)
        core_copy(s).wait_recv()
        acc[s] = x[s, core] + c_in[s]

        @pl.when(z < mid)
        def _():
            from_lower(s)
            up(s).start()

        @pl.when(z > mid)
        def _():
            from_upper(s)
            down(s).start()

    def total(s):
        @pl.when(z == centre(s))
        def _():
            from_lower(s)
            from_upper(s)
            out[s, core] = acc[s]

            @pl.when(has_l)
            def _():
                final_down(s).start()

            @pl.when(has_r)
            def _():
                final_up(s).start()

            share(s).start()

    def spread(s):
        mid = centre(s)

        @pl.when(z < mid)
        def _():
            final_down(s).wait_recv()

            @pl.when(has_l)
            def _():
                final_down(s).start()

            share(s).start()

        @pl.when(z > mid)
        def _():
            final_up(s).wait_recv()

            @pl.when(has_r)
            def _():
                final_up(s).start()

            share(s).start()

    def loop(lo, hi, body):
        def step(s, carry):
            body(s)
            return carry

        lax.fori_loop(lo, hi, step, 0)

    def stages(lags):
        def body(i):
            for work, lag in lags:

                @pl.when(jnp.logical_and(i >= lag, i < n + lag))
                def _():
                    work(i - lag)

        loop(0, n + max(lag for _, lag in lags), body)

    if nz > 2:
        end = jnp.logical_or(z == 0, z == nz - 1)

        @pl.when(end)
        def _():
            stages([(product, 0), (forward, 2)])
            loop(0, n, spread)

        @pl.when(jnp.logical_not(end))
        def _():
            stages([(product, 0), (forward, 2), (total, 4), (spread, 6)])

    else:
        stages([(product, 0), (forward, 2), (total, 4), (spread, 6)])

    def drain(s):
        mid = centre(s)
        core_copy(s).wait_send()

        @pl.when(z != mid)
        def _():
            up(s).wait_send()

        @pl.when(jnp.logical_and(z <= mid, has_l))
        def _():
            final_down(s).wait_send()

        @pl.when(jnp.logical_and(z >= mid, has_r))
        def _():
            final_up(s).wait_send()

        share(s).wait_send()
        share_in(s).wait_recv()

    loop(0, n, drain)

    def square(s, carry):
        v = out[s].reshape(RANK, tile)
        for k in range(tile // 128):
            w = v[:, k * 128 : (k + 1) * 128]
            carry = carry + w * w
        return carry

    squares = lax.fori_loop(0, n, square, jnp.zeros((RANK, 128), F32))
    sqs[0] = jnp.broadcast_to(jnp.sum(squares.T, axis=0, keepdims=True), (8, RANK))
    sends = [copy(sqs.at[0], sqs.at[d], ss.at[d - 1], sr.at[d - 1], cols[d], "col") for d in range(1, nc)]
    for c in sends:
        c.start()
    total_sq = sqs[0]
    for d in range(1, nc):
        sends[d - 1].wait_recv()
        total_sq = total_sq + sqs[d]
    for c in sends:
        c.wait_send()
    sq[...] = total_sq


def right_total(g, m, t, nr, nc):
    rows, cols = g.shape
    tile = min(tile_of(cols), 256)
    n = cols // tile
    vm = pl.BlockSpec(memory_space=VMEM)
    hbm = pl.BlockSpec(memory_space=pl.ANY)
    piece = VMEM((n, RANK // 2, tile), F32)
    out, sq = pl.pallas_call(
        functools.partial(right_kernel, nr, nc),
        in_specs=[hbm, hbm, vm],
        out_specs=[vm, vm],
        out_shape=[
            jax.ShapeDtypeStruct((n, 2, RANK // 2, tile), F32),
            jax.ShapeDtypeStruct((8, RANK), F32),
        ],
        scratch_shapes=[
            VMEM((2, rows, tile), BF16),
            VMEM((2, rows, tile), BF16),
            VMEM((n, 2, RANK // 2, tile), F32),
            piece,
            piece,
            piece,
            piece,
            VMEM((nc, 8, RANK), F32),
        ]
        + [DMA((2,))] * 2
        + [DMA((n,))] * 10
        + [DMA((nc - 1,))] * 2,
        compiler_params=pltpu.CompilerParams(
            collective_id=1, has_side_effects=True, vmem_limit_bytes=LIMIT
        ),
    )(g, m, t)
    return out.reshape(n, RANK, tile), sq


def final_kernel(scale, g_ref, m_ref, w_ref, o_ref, rt_ref, sq_ref, nw_ref, nm_ref, nf_ref):
    rt = jnp.concatenate([rt_ref[k] for k in range(rt_ref.shape[0])], axis=1)
    ft = rt / jnp.sqrt(sq_ref[...].T[:, :1] / COLS + 1e-06)
    nf_ref[...] = ft.T
    buffer = g_ref[...].astype(F32) + m_ref[...].astype(F32)
    nm_ref[...] = (buffer - mm(o_ref[:, :RANK], ((1.0 - decay) * rt).astype(BF16))).astype(BF16)
    f_hi, f_lo = split(scale * ft)
    update = mm(o_ref[...], jnp.concatenate([f_hi, f_hi, f_lo], axis=0))
    nw_ref[...] = (w_ref[...].astype(F32) - update).astype(BF16)


def final(g, m, w, o, rt, sq):
    rows, cols = g.shape
    tile = tile_of(cols)
    block = pl.BlockSpec((rows, tile), lambda i: (0, i))
    return pl.pallas_call(
        functools.partial(final_kernel, step_size * (ROWS / RANK) ** 0.5),
        grid=(cols // tile,),
        in_specs=[
            block,
            block,
            block,
            whole((rows, 3 * RANK)),
            pl.BlockSpec((tile // rt.shape[2], RANK, rt.shape[2]), lambda i: (i, 0, 0)),
            whole((8, RANK)),
        ],
        out_specs=[block, block, pl.BlockSpec((tile, RANK), lambda i: (i, 0))],
        out_shape=[
            jax.ShapeDtypeStruct((rows, cols), BF16),
            jax.ShapeDtypeStruct((rows, cols), BF16),
            jax.ShapeDtypeStruct((cols, RANK), F32),
        ],
        compiler_params=pltpu.CompilerParams(vmem_limit_bytes=LIMIT),
    )(g, m, w, o, rt, sq)


def local(nr, nc, gradient, momentum, weight, right_factor):
    part = left_part(gradient, momentum, right_factor)
    left, gram = sums(part, nr, nc)
    o, t = ortho_of(gram, left)
    rt, sq = right_total(gradient, momentum, t, nr, nc)
    return tuple(final(gradient, momentum, weight, o, rt, sq))


def solution(mesh):
    in_specs = (P("row", "col"), P("row", "col"), P("row", "col"), P("col", None))
    out_specs = (P("row", "col"), P("row", "col"), P("col", None))
    body = functools.partial(local, mesh.shape["row"], mesh.shape["col"])
    return jax.shard_map(body, mesh=mesh, in_specs=in_specs, out_specs=out_specs, check_vma=False)
```
